32 devices in a mesh: batch: 4 (over y, x), ctx: 8 (over z, core).
Axes of the slice: x: 2, y: 2, z: 4, core: 2. Of those that a mesh axis runs over, the one named last changes fastest.
Arguments:
- inner_x: bfloat16 [4, 512, 8192], P('batch', 'ctx'), may hold values from -6 to 6
- inner_bc: bfloat16 [4, 512, 1024], P('batch', 'ctx'), may hold values from -6 to 6
- step_size: float32 [4, 512, 64], P('batch', 'ctx'), may hold values from 0.1 to 1400, as said below
- decay_base: float32 [64], replicated, may hold values from 0.9995 to 0.9998
- conv_inner: float32 [4, 8192], replicated, may hold values from -3 to 3
- conv_groups: float32 [4, 1024], replicated, may hold values from -3 to 3
- norm_gain: float32 [8192], replicated, may hold values from 0.5 to 1.5
- cache_pool: bfloat16 [16, 64, 128, 128], P('batch', 'ctx'), may hold values from -0.59765625 to 0.59765625
- reuse_owner: int32 [4], replicated, may hold values from 0 to 3
- reuse_level: int32 [4], replicated, may hold values from 0 to 4, as said below
- prompt_blocks: int32 [4], replicated, may hold values from 1 to 2
Outputs:
- mixer_out: bfloat16 [4, 512, 8192], P('batch', 'ctx')
The draws below stay inside these ranges and needn't reach their ends.
Inputs may be any that keep to these rules, and one draw needn't show every extreme that they name: `step_size`: positive step sizes. `reuse_level`: 0 means nothing is cached; level l names the owner's l-th cached state.
All inputs are finite; a program needn't handle non-finite values.
Results may differ from the reference program's by a relative error of at most 0.009.
Values may be sent and summed in bfloat16 or wider, within the bound.
A program may use at most 64 MiB of HBM per device.

```python
import math
import jax
import jax.numpy as jnp
import numpy as np
from jax import lax

LOCAL_HEADS = 64
P_SIZE = 128
N = 128
GROUPS = 4
KCONV = 4
TOK_DEV = 64
SLOTS = 4
LEN_BLOCK = 256
PROMPT_LENGTH = 512
REQUEST_COUNT = 4
N_CTX = 8


def draw_step_size(key, part):
    random_key_parts = jax.random.split(key, 4)
    fast_heads = jax.random.randint(random_key_parts[0], (LOCAL_HEADS,), 0, 4) == 0
    roughness = jax.random.uniform(random_key_parts[1], (REQUEST_COUNT, PROMPT_LENGTH, LOCAL_HEADS), jnp.float32)
    baseline_step = jnp.where(fast_heads[None, None, :], 40.0 + 60.0 * roughness, 0.1 + 0.4 * roughness)
    spike_position = jax.random.randint(random_key_parts[2], (REQUEST_COUNT, 2), 0, PROMPT_LENGTH)
    spike_applied = jnp.any(jnp.arange(PROMPT_LENGTH)[None, :, None] == spike_position[:, None, :], axis=2)
    spike_step_size = 800.0 + 600.0 * jax.random.uniform(random_key_parts[3], (REQUEST_COUNT, PROMPT_LENGTH, LOCAL_HEADS), jnp.float32)
    return jnp.where(spike_applied[:, :, None], spike_step_size, baseline_step).astype(jnp.float32)


def draw_reuse_level(key, part):
    random_key_parts = jax.random.split(key, 2)
    cached_level = jax.random.randint(random_key_parts[0], (REQUEST_COUNT,), 0, SLOTS + 1)
    first = jax.random.randint(random_key_parts[1], (), 0, REQUEST_COUNT)
    cached_level = cached_level.at[first].set(SLOTS)
    cached_level = cached_level.at[(first + 1) % REQUEST_COUNT].set(0)
    return cached_level.astype(jnp.int32)


def draw_prompt_blocks(key, part):
    random_key_parts = jax.random.split(key, 2)
    most_blocks = PROMPT_LENGTH // LEN_BLOCK
    length_blocks = jax.random.randint(random_key_parts[0], (REQUEST_COUNT,), max(most_blocks // 4, 1), most_blocks + 1)
    first = jax.random.randint(random_key_parts[1], (), 0, REQUEST_COUNT)
    length_blocks = length_blocks.at[first].set(most_blocks)
    return length_blocks.astype(jnp.int32)


def plant(values, stream_key, low, largest):
    extent = values.shape
    spot = [jax.random.randint(jax.random.fold_in(stream_key, axis), (), 0, extent[axis]) for axis in range(len(extent))]
    values = values.at[tuple(spot)].set(low)
    longest = extent.index(max(extent))
    spot[longest] = (spot[longest] + 1) % extent[longest]
    return values.at[tuple(spot)].set(largest)


def shard_levels(stream_key, extent, shards, smallest, high):
    factor_of, own = 1.0, jax.random.fold_in(stream_key, 6)
    for axis_at, blocks in shards:
        heights = jnp.exp(jax.random.uniform(jax.random.fold_in(own, axis_at), (blocks,), jnp.float32, smallest / len(shards), high / len(shards)))
        factor_of = factor_of * jnp.repeat(heights, extent[axis_at] // blocks).reshape([-1 if axis == axis_at else 1 for axis in range(len(extent))])
    return factor_of


def rank_table(number_of, lean):
    portions = [(1 << 20) // math.isqrt(grade ** lean) + 1 for grade in range(1, number_of + 1)]
    deviation = 1 + sum(portions) // (1 << 30)
    return np.cumsum(np.array([max(1, weight // deviation) for weight in portions]))


def ranked(stream_key, extent, number_of, lean):
    grid = rank_table(number_of, lean)
    pick = jax.random.randint(jax.random.fold_in(stream_key, 1), extent, 0, int(grid[number_of - 1]))
    standing = jnp.searchsorted(jnp.asarray(grid, jnp.int32), pick, side="right")
    return jax.random.permutation(jax.random.fold_in(stream_key, 2), number_of)[standing].astype(jnp.int32)


def normal_values(stream_key, extent, width, limit, cuts=(), kind=jnp.bfloat16):
    values = jax.random.normal(stream_key, extent, jnp.float32) * width
    if len(cuts) > 0:
        values = shard_levels(stream_key, extent, cuts, -0.22, 0.18) * values
    return jnp.clip(values, min=-limit, max=limit).astype(kind)


def setup_inputs(seed: int = 0) -> dict:
    splits = jax.random.split(jax.random.key(seed), 12)
    return {
        "inner_x": normal_values(splits[0], (REQUEST_COUNT, PROMPT_LENGTH, LOCAL_HEADS * P_SIZE), 1.0, 6.0, ((0, 4), (1, 8))),
        "inner_bc": normal_values(splits[1], (REQUEST_COUNT, PROMPT_LENGTH, 2 * GROUPS * N), 1.0, 6.0, ((0, 4), (1, 8))),
        "step_size": draw_step_size(jax.random.fold_in(splits[11], 71), 0),
        "decay_base": jnp.clip(jax.random.uniform(splits[3], (LOCAL_HEADS,), jnp.float32, 0.9995, 0.9998), 0.9995, 0.9998),
        "conv_inner": normal_values(splits[4], (KCONV, LOCAL_HEADS * P_SIZE), KCONV ** -0.5, 3.0, (), jnp.float32),
        "conv_groups": normal_values(splits[5], (KCONV, 2 * GROUPS * N), KCONV ** -0.5, 3.0, (), jnp.float32),
        "norm_gain": jnp.clip(1.0 + 0.1 * jax.random.normal(splits[6], (LOCAL_HEADS * P_SIZE,), jnp.float32), 0.5, 1.5),
        "cache_pool": normal_values(splits[7], (REQUEST_COUNT * SLOTS, LOCAL_HEADS, P_SIZE, N), 0.1, 0.59765625, ((0, 4), (1, 8))),
        "reuse_owner": plant(ranked(splits[8], (REQUEST_COUNT,), REQUEST_COUNT, 2), jax.random.fold_in(splits[8], 3), 0, REQUEST_COUNT - 1).astype(jnp.int32),
        "reuse_level": draw_reuse_level(jax.random.fold_in(splits[11], 71), 0),
        "prompt_blocks": draw_prompt_blocks(jax.random.fold_in(splits[11], 71), 0),
    }


def conv_silu(values, weight):
    kernel = weight.shape[0]
    length = values.shape[0]
    padded = jnp.pad(values, ((kernel - 1, 0), (0, 0)))
    summed = jnp.zeros(values.shape, jnp.float32)
    for offset in range(kernel):
        summed = summed + weight[offset] * padded[offset:offset + length].astype(jnp.float32)
    return jax.nn.silu(summed).astype(jnp.bfloat16)

def block_local(conv_x, write_proj, read_proj, log_step):
    length = log_step.shape[0]
    per_group = LOCAL_HEADS // GROUPS
    cumul = jnp.cumsum(log_step, axis=0)
    inject = -jnp.expm1(log_step)
    inner_heads = conv_x.reshape(length, GROUPS, per_group, P_SIZE).astype(jnp.float32)
    write_groups = write_proj.reshape(length, GROUPS, N).astype(jnp.float32)
    read_groups = read_proj.reshape(length, GROUPS, N).astype(jnp.float32)
    scores = jnp.einsum('tgn,sgn->gts', read_groups, write_groups)
    row_index = jnp.arange(length)[:, None]
    col_index = jnp.arange(length)[None, :]
    cumul_heads = cumul.T.reshape(GROUPS, per_group, length)
    inject_heads = inject.T.reshape(GROUPS, per_group, length)
    exponent_gap = cumul_heads[:, :, :, None] - cumul_heads[:, :, None, :]
    exponent_gap = jnp.where(row_index >= col_index, exponent_gap, -jnp.inf)
    mixing = (scores[:, None] * jnp.exp(exponent_gap) * inject_heads[:, :, None, :]).astype(jnp.bfloat16)
    intra_part = jnp.einsum('gkts,sgkp->tgkp', mixing.astype(jnp.float32), inner_heads)
    tail_weight = jnp.exp(cumul[-1][None, :] - cumul) * inject
    weighted = (inner_heads * tail_weight.reshape(length, GROUPS, per_group)[..., None]).astype(jnp.bfloat16)
    end_state = jnp.einsum('sgkp,sgn->gkpn', weighted.astype(jnp.float32), write_groups)
    end_state = end_state.reshape(LOCAL_HEADS, P_SIZE, N).astype(jnp.bfloat16)
    block_decay = jnp.exp(cumul[-1]).astype(jnp.bfloat16)
    return (intra_part.reshape(length, LOCAL_HEADS, P_SIZE), cumul, end_state, block_decay)

def block_output(intra_part, cumul, read_proj, incoming, norm_gain, live):
    length = cumul.shape[0]
    per_group = LOCAL_HEADS // GROUPS
    read_groups = read_proj.reshape(length, GROUPS, N).astype(jnp.float32)
    state_groups = incoming.reshape(GROUPS, per_group, P_SIZE, N).astype(jnp.float32)
    inter_part = jnp.einsum('tgn,gkpn->tgkp', read_groups, state_groups).reshape(length, LOCAL_HEADS, P_SIZE)
    summed = intra_part + jnp.exp(cumul)[:, :, None] * inter_part
    inv_scale = lax.rsqrt(lax.optimization_barrier(jnp.mean(summed * summed, axis=2, keepdims=True)) + 1e-05)
    result = summed * inv_scale * norm_gain.reshape(LOCAL_HEADS, P_SIZE)
    result = jnp.where(live[:, None, None], result, 0.0)
    return result.reshape(length, LOCAL_HEADS * P_SIZE).astype(jnp.bfloat16)

def reference(inner_x, inner_bc, step_size, decay_base, conv_inner, conv_groups, norm_gain, cache_pool, reuse_owner, reuse_level, prompt_blocks):

    def one_request(request_args):
        x_tokens, bc_tokens, dt_tokens, cache_owner, cached_level, length_blocks = request_args
        conv_x = conv_silu(x_tokens, conv_inner)
        conv_bc = conv_silu(bc_tokens, conv_groups)
        positions = jnp.arange(PROMPT_LENGTH)
        live = positions < length_blocks * LEN_BLOCK
        log_step = jnp.where(live[:, None], dt_tokens, 0.0) * jnp.log(decay_base)[None, :]
        slot_index = (cache_owner * SLOTS + jnp.maximum(cached_level - 1, 0)).astype(jnp.int32)
        start_state = lax.dynamic_index_in_dim(cache_pool, slot_index, 0, keepdims=False).astype(jnp.float32)
        start_state = jnp.where(cached_level > 0, start_state, 0.0)
        blocks = (conv_x.reshape(N_CTX, TOK_DEV, LOCAL_HEADS * P_SIZE), conv_bc.reshape(N_CTX, TOK_DEV, 2 * GROUPS * N), log_step.reshape(N_CTX, TOK_DEV, LOCAL_HEADS), live.reshape(N_CTX, TOK_DEV))

        def block_step(running, pieces):
            x_block, bc_block, step_block, live_block = pieces
            intra_part, cumul, end_state, block_decay = block_local(x_block, bc_block[:, :GROUPS * N], bc_block[:, GROUPS * N:], step_block)
            result = block_output(intra_part, cumul, bc_block[:, GROUPS * N:], running.astype(jnp.bfloat16), norm_gain, live_block)
            next_state = block_decay.astype(jnp.float32)[:, None, None] * running + end_state.astype(jnp.float32)
            return (next_state, result)
        last_state, outputs = lax.scan(block_step, start_state, blocks)
        return outputs.reshape(PROMPT_LENGTH, LOCAL_HEADS * P_SIZE)
    return lax.map(one_request, (inner_x, inner_bc, step_size, reuse_owner, reuse_level, prompt_blocks))
```

```python
import functools

import jax
import jax.numpy as jnp
from jax import lax
from jax.experimental import pallas as pl
from jax.experimental.pallas import tpu as pltpu
from jax.sharding import PartitionSpec as P

LOCAL_HEADS = 64
P_SIZE = 128
N = 128
GROUPS = 4
KCONV = 4
LEN_BLOCK = 256
HALO = 16
F32 = jnp.float32
BF16 = jnp.bfloat16
MESH = pl.DeviceIdType.MESH
NT = (((1,), (1,)), ((), ()))
TN = (((0,), (0,)), ((), ()))


def one_minus_exp(value):
    total = jnp.ones_like(value)
    for term in range(12, 1, -1):
        total = 1.0 + value * (1.0 / term) * total
    return -value * total


def convolved(ext_ref, weight, length, width):
    summed = jnp.zeros((length, width), F32)
    for offset in range(KCONV):
        start = 8 - (KCONV - 1) + offset
        summed = summed + weight[offset : offset + 1] * ext_ref[start : start + length, :width]
    return (summed * jax.nn.sigmoid(summed)).astype(BF16)


def kernel(
    nb, nc, length,
    owner_ref, level_ref, blocks_ref,
    x_ref, bc_ref, step_ref, stept_ref, base_ref, baset_ref, wx_ref, wbc_ref, gain_ref, pool_ref,
    out_ref,
    hx, hbc, ext, bcv, colc, coli, rowc, rowi, intra, ends, inc, nxt, sel_out, sel_in, start,
    halo_send, halo_recv, sel_send, sel_recv, st_send, inc_recv, nxt_send,
):
    hs = LOCAL_HEADS // nc
    width = hs * P_SIZE
    per_group = LOCAL_HEADS // GROUPS
    me_b = lax.axis_index("batch")
    me_c = lax.axis_index("ctx")
    live_count = blocks_ref[me_b] * LEN_BLOCK

    barrier = pltpu.get_barrier_semaphore()
    for step in range(1, nb):
        pl.semaphore_signal(barrier, inc=1, device_id=(lax.rem(me_b + step, nb), me_c), device_id_type=MESH)
    for step in range(1, nc):
        pl.semaphore_signal(barrier, inc=1, device_id=(me_b, lax.rem(me_c + step, nc)), device_id_type=MESH)

    def pick(request):
        return pool_ref[jnp.maximum(level_ref[request] - 1, 0)].reshape(width, N)

    for step in range(1, nb):
        sel_out[step - 1] = pick(lax.rem(me_b + step, nb))
    own = pick(me_b)
    pl.semaphore_wait(barrier, nb - 1 + nc - 1)

    def halo_copy(which):
        source, target = ((x_ref, hx), (bc_ref, hbc))[which]
        return pltpu.make_async_remote_copy(
            src_ref=source.at[pl.ds(length - HALO, HALO)], dst_ref=target,
            send_sem=halo_send.at[which], recv_sem=halo_recv.at[which],
            device_id=(me_b, lax.rem(me_c + 1, nc)), device_id_type=MESH,
        )

    def sel_copy(step):
        return pltpu.make_async_remote_copy(
            src_ref=sel_out.at[step - 1], dst_ref=sel_in.at[step - 1],
            send_sem=sel_send.at[step - 1], recv_sem=sel_recv.at[step - 1],
            device_id=(lax.rem(me_b + step, nb), me_c), device_id_type=MESH,
        )

    def start_copy():
        return pltpu.make_async_remote_copy(
            src_ref=start, dst_ref=inc.at[me_c],
            send_sem=st_send, recv_sem=inc_recv.at[me_c],
            device_id=(me_b, 0), device_id_type=MESH,
        )

    def next_copy(k):
        return pltpu.make_async_remote_copy(
            src_ref=nxt.at[k], dst_ref=inc.at[k],
            send_sem=nxt_send.at[k], recv_sem=inc_recv.at[k],
            device_id=(me_b, lax.rem(me_c + 1, nc)), device_id_type=MESH,
        )

    @pl.when(me_c < nc - 1)
    def _():
        halo_copy(1).start()
        halo_copy(0).start()

    for step in range(1, nb):
        sel_copy(step).start()

    first = me_c * length
    row_at = lax.broadcasted_iota(jnp.int32, (length, LOCAL_HEADS), 0)
    col_at = lax.broadcasted_iota(jnp.int32, (LOCAL_HEADS, length), 1)
    logs = jnp.where(first + row_at < live_count, step_ref[...], 0.0) * jnp.log(base_ref[...])
    logst = jnp.where(first + col_at < live_count, stept_ref[...], 0.0) * jnp.log(baset_ref[...])
    at_t = lax.broadcasted_iota(jnp.int32, (length, length), 0)
    at_s = lax.broadcasted_iota(jnp.int32, (length, length), 1)
    causal = at_t >= at_s
    lower = causal.astype(F32)
    upper = (at_t <= at_s).astype(F32)
    cum = jnp.dot(lower, logs, precision=lax.Precision.HIGHEST, preferred_element_type=F32)
    cumt = jnp.dot(logst, upper, precision=lax.Precision.HIGHEST, preferred_element_type=F32)
    tail = jnp.exp(cum[length - 1 : length] - cum) * one_minus_exp(logs)
    injt = one_minus_exp(logst)
    for k in range(nc):
        colc[k] = cum[:, k * hs : (k + 1) * hs]
        coli[k] = tail[:, k * hs : (k + 1) * hs]
        rowc[k] = cumt[k * hs : (k + 1) * hs]
        rowi[k] = injt[k * hs : (k + 1) * hs]

    @pl.when(me_c == 0)
    def _():
        hx[...] = jnp.zeros_like(hx)
        hbc[...] = jnp.zeros_like(hbc)

    @pl.when(me_c > 0)
    def _():
        halo_copy(1).wait_recv()
        halo_copy(0).wait_recv()

    half = GROUPS * N
    for part in range(2):
        cols = slice(part * half, (part + 1) * half)
        for piece in range(GROUPS):
            at = part * half + piece * N
            ext[0:8, :N] = hbc[:, at : at + N].astype(F32)[HALO - 8 :]
            ext[8 : 8 + length, :N] = bc_ref[:, at : at + N].astype(F32)
            bcv[part * GROUPS + piece] = convolved(ext, wbc_ref[:, at : at + N], length, N)

    def local_part(k, carry):
        group = k * hs // per_group
        cols = pl.ds(pl.multiple_of(k * width, 128), width)
        write = bcv[group]
        read = bcv[GROUPS + group]
        scores = lax.dot_general(read, write, NT, preferred_element_type=F32)
        col_c, col_i, row_c, row_i = colc[k], coli[k], rowc[k], rowi[k]
        ext[0:8, :width] = hx[:, cols].astype(F32)[HALO - 8 :]
        ext[8 : 8 + length, :width] = x_ref[:, cols].astype(F32)
        conv = convolved(ext, wx_ref[:, cols], length, width)
        outs, weighted = [], []
        for j in range(hs):
            head = conv[:, j * P_SIZE : (j + 1) * P_SIZE]
            gap = jnp.where(causal, col_c[:, j : j + 1] - row_c[j : j + 1], -jnp.inf)
            mixing = (scores * jnp.exp(gap) * row_i[j : j + 1]).astype(BF16)
            outs.append(jnp.dot(mixing, head, preferred_element_type=F32))
            weighted.append((head.astype(F32) * col_i[:, j : j + 1]).astype(BF16))
        intra[k] = jnp.concatenate(outs, axis=1)
        stacked = jnp.concatenate(weighted, axis=1)
        ends[k] = lax.dot_general(stacked, write, TN, preferred_element_type=F32).astype(BF16)
        return carry

    lax.fori_loop(0, nc, local_part, 0)

    owner = owner_ref[me_b]
    level = level_ref[me_b]
    state = jnp.where(owner == me_b, own, jnp.zeros_like(own))
    for step in range(1, nb):
        sel_copy(step).wait_recv()
        state = jnp.where(owner == lax.rem(me_b + nb - step, nb), sel_in[step - 1], state)
    state = jnp.where(level > 0, state, jnp.zeros_like(state))

    @pl.when(me_c == 0)
    def _():
        inc[0] = state

    @pl.when(me_c > 0)
    def _():
        start[...] = state
        start_copy().start()

    def chain_part(k, carry):
        @pl.when(me_c + k > 0)
        def _():
            next_copy(k).wait_recv()

        row_c = rowc[k]
        decay = jnp.exp(row_c[:, length - 1 : length]).astype(BF16).astype(F32)

        @pl.when(me_c < nc - 1)
        def _():
            for j in range(hs):
                rows = slice(j * P_SIZE, (j + 1) * P_SIZE)
                nxt[k, rows] = (
                    decay[j : j + 1] * inc[k, rows].astype(F32) + ends[k, rows].astype(F32)
                ).astype(BF16)
            next_copy(k).start()

        cols = pl.ds(pl.multiple_of(k * width, 128), width)
        read = bcv[GROUPS + k * hs // per_group]
        inter = lax.dot_general(read, inc[k], NT, preferred_element_type=F32)
        grown = jnp.exp(colc[k])
        gain = gain_ref[:, cols]
        alive = first + lax.broadcasted_iota(jnp.int32, (length, P_SIZE), 0) < live_count
        outs = []
        for j in range(hs):
            lanes = slice(j * P_SIZE, (j + 1) * P_SIZE)
            summed = intra[k, :, lanes] + grown[:, j : j + 1] * inter[:, lanes]
            scale = lax.rsqrt(jnp.mean(summed * summed, axis=1, keepdims=True) + 1e-05)
            outs.append(jnp.where(alive, summed * scale * gain[:, lanes], 0.0).astype(BF16))
        out_ref[:, cols] = jnp.concatenate(outs, axis=1)
        return carry

    lax.fori_loop(0, nc, chain_part, 0)

    for step in range(1, nb):
        sel_copy(step).wait_send()

    @pl.when(me_c > 0)
    def _():
        start_copy().wait_send()

    @pl.when(me_c < nc - 1)
    def _():
        halo_copy(1).wait_send()
        halo_copy(0).wait_send()

        def drain(k, carry):
            next_copy(k).wait_send()
            return carry

        lax.fori_loop(0, nc, drain, 0)


def body(
    nb, nc,
    inner_x, inner_bc, step_size, decay_base, conv_inner, conv_groups, norm_gain, cache_pool,
    reuse_owner, reuse_level, prompt_blocks,
):
    length, width_x = inner_x.shape[1:]
    width_bc = inner_bc.shape[2]
    hs = LOCAL_HEADS // nc
    width = hs * P_SIZE
    smem = pl.BlockSpec(memory_space=pltpu.SMEM)
    vmem = pl.BlockSpec(memory_space=pltpu.VMEM)
    dma = pltpu.SemaphoreType.DMA
    result = pl.pallas_call(
        functools.partial(kernel, nb, nc, length),
        out_shape=jax.ShapeDtypeStruct((length, width_x), BF16),
        in_specs=[smem] * 3 + [vmem] * 10,
        out_specs=vmem,
        scratch_shapes=[
            pltpu.VMEM((HALO, width_x), BF16),
            pltpu.VMEM((HALO, width_bc), BF16),
            pltpu.VMEM((8 + length, max(width, N)), F32),
            pltpu.VMEM((2 * GROUPS, length, N), BF16),
            pltpu.VMEM((nc, length, hs), F32),
            pltpu.VMEM((nc, length, hs), F32),
            pltpu.VMEM((nc, hs, length), F32),
            pltpu.VMEM((nc, hs, length), F32),
            pltpu.VMEM((nc, length, width), F32),
            pltpu.VMEM((nc, width, N), BF16),
            pltpu.VMEM((nc, width, N), BF16),
            pltpu.VMEM((nc, width, N), BF16),
            pltpu.VMEM((nb - 1, width, N), BF16),
            pltpu.VMEM((nb - 1, width, N), BF16),
            pltpu.VMEM((width, N), BF16),
            dma((2,)),
            dma((2,)),
            dma((nb - 1,)),
            dma((nb - 1,)),
            dma,
            dma((nc,)),
            dma((nc,)),
        ],
        compiler_params=pltpu.CompilerParams(
            collective_id=0, has_side_effects=True, vmem_limit_bytes=40 * 1024 * 1024
        ),
    )(
        reuse_owner, reuse_level, prompt_blocks,
        inner_x[0], inner_bc[0], step_size[0], step_size[0].T,
        decay_base[None, :], decay_base[:, None], conv_inner, conv_groups, norm_gain[None, :],
        cache_pool,
    )
    return result[None]


def solution(mesh):
    return jax.shard_map(
        functools.partial(body, mesh.shape["batch"], mesh.shape["ctx"]),
        mesh=mesh,
        in_specs=(
            P("batch", "ctx", None),
            P("batch", "ctx", None),
            P("batch", "ctx", None),
            P(),
            P(),
            P(),
            P(),
            P("batch", "ctx", None, None),
            P(),
            P(),
            P(),
        ),
        out_specs=P("batch", "ctx", None),
        check_vma=False,
    )
```

```python
import functools

import jax
import jax.numpy as jnp
from jax import lax
from jax.experimental import pallas as pl
from jax.experimental.pallas import tpu as pltpu
from jax.sharding import PartitionSpec as P

LOCAL_HEADS = 64
P_SIZE = 128
N = 128
GROUPS = 4
KCONV = 4
LEN_BLOCK = 256
HALO = 16
PARTS = 2
F32 = jnp.float32
BF16 = jnp.bfloat16
MESH = pl.DeviceIdType.MESH
NT = (((1,), (1,)), ((), ()))
TN = (((0,), (0,)), ((), ()))


def one_minus_exp(value):
    total = jnp.ones_like(value)
    for term in range(12, 1, -1):
        total = 1.0 + value * (1.0 / term) * total
    return -value * total


def convolved(ext_ref, weight, length, width):
    summed = jnp.zeros((length, width), F32)
    for offset in range(KCONV):
        start = 8 - (KCONV - 1) + offset
        summed = summed + weight[offset : offset + 1] * ext_ref[start : start + length, :width]
    return (summed * jax.nn.sigmoid(summed)).astype(BF16)


def kernel(
    nb, nc, length,
    owner_ref, level_ref, blocks_ref,
    x_hbm, bc_ref, step_ref, base_ref, wx_hbm, wbc_ref, gain_ref, pool_hbm,
    out_ref,
    x_ref, wx_ref, pool_ref, convs,
    hx, hbc, ext, bcv, colc, coli, rowc, rowi, intra, ends, inc, nxt, sel_out, sel_in, start,
    local_sem, halo_send, halo_recv, sel_send, sel_recv, st_send, inc_recv, nxt_send,
):
    hs = LOCAL_HEADS // nc
    width = hs * P_SIZE
    sub = width // PARTS
    per_group = LOCAL_HEADS // GROUPS
    me_b = lax.axis_index("batch")
    me_c = lax.axis_index("ctx")
    live_count = blocks_ref[me_b] * LEN_BLOCK

    loads = [
        pltpu.make_async_copy(source, target, local_sem.at[at])
        for at, (source, target) in enumerate(((pool_hbm, pool_ref), (x_hbm, x_ref), (wx_hbm, wx_ref)))
    ]
    for load in loads:
        load.start()
    barrier = pltpu.get_barrier_semaphore()
    for step in range(1, nb):
        pl.semaphore_signal(barrier, inc=1, device_id=(lax.rem(me_b + step, nb), me_c), device_id_type=MESH)
    for step in range(1, nc):
        pl.semaphore_signal(barrier, inc=1, device_id=(me_b, lax.rem(me_c + step, nc)), device_id_type=MESH)

    loads[0].wait()

    def pick(request):
        return pool_ref[jnp.maximum(level_ref[request] - 1, 0)].reshape(width, N)

    for step in range(1, nb):
        sel_out[step - 1] = pick(lax.rem(me_b + step, nb))
    start[...] = pick(me_b)
    loads[1].wait()
    pl.semaphore_wait(barrier, nb - 1 + nc - 1)

    def halo_copy(which):
        source, target = ((x_ref, hx), (bc_ref, hbc))[which]
        return pltpu.make_async_remote_copy(
            src_ref=source.at[pl.ds(length - HALO, HALO)], dst_ref=target,
            send_sem=halo_send.at[which], recv_sem=halo_recv.at[which],
            device_id=(me_b, lax.rem(me_c + 1, nc)), device_id_type=MESH,
        )

    def sel_copy(step):
        return pltpu.make_async_remote_copy(
            src_ref=sel_out.at[step - 1], dst_ref=sel_in.at[step - 1],
            send_sem=sel_send.at[step - 1], recv_sem=sel_recv.at[step - 1],
            device_id=(lax.rem(me_b + step, nb), me_c), device_id_type=MESH,
        )

    def start_copy(part):
        rows = pl.ds(part * sub, sub)
        return pltpu.make_async_remote_copy(
            src_ref=start.at[rows], dst_ref=inc.at[me_c, rows],
            send_sem=st_send.at[part], recv_sem=inc_recv.at[me_c, part],
            device_id=(me_b, 0), device_id_type=MESH,
        )

    def next_copy(k, part):
        rows = pl.ds(part * sub, sub)
        return pltpu.make_async_remote_copy(
            src_ref=nxt.at[k, rows], dst_ref=inc.at[k, rows],
            send_sem=nxt_send.at[k, part], recv_sem=inc_recv.at[k, part],
            device_id=(me_b, lax.rem(me_c + 1, nc)), device_id_type=MESH,
        )

    @pl.when(me_c < nc - 1)
    def _():
        halo_copy(1).start()
        halo_copy(0).start()

    for step in range(1, nb):
        sel_copy(step).start()

    first = me_c * length
    row_at = lax.broadcasted_iota(jnp.int32, (length, LOCAL_HEADS), 0)
    logs = jnp.where(first + row_at < live_count, step_ref[...], 0.0) * jnp.log(base_ref[...])
    at_t = lax.broadcasted_iota(jnp.int32, (length, length), 0)
    at_s = lax.broadcasted_iota(jnp.int32, (length, length), 1)
    causal = at_t >= at_s
    lower = causal.astype(F32)
    upper = (at_t <= at_s).astype(F32)
    cum = jnp.dot(lower, logs, precision=lax.Precision.HIGHEST, preferred_element_type=F32)
    cumt = lax.dot_general(logs, upper, TN, precision=lax.Precision.HIGHEST, preferred_element_type=F32)
    inject = one_minus_exp(logs)
    tail = jnp.exp(cum[length - 1 : length] - cum) * inject
    same = (at_t == at_s).astype(F32)
    injt = lax.dot_general(inject, same, TN, precision=lax.Precision.HIGHEST, preferred_element_type=F32)
    for k in range(nc):
        colc[k] = cum[:, k * hs : (k + 1) * hs]
        coli[k] = tail[:, k * hs : (k + 1) * hs]
        rowc[k] = cumt[k * hs : (k + 1) * hs]
        rowi[k] = injt[k * hs : (k + 1) * hs]

    @pl.when(me_c == 0)
    def _():
        hx[...] = jnp.zeros_like(hx)
        hbc[...] = jnp.zeros_like(hbc)

    @pl.when(me_c > 0)
    def _():
        halo_copy(1).wait_recv()
        halo_copy(0).wait_recv()

    half = GROUPS * N
    for part in range(2):
        cols = slice(part * half, (part + 1) * half)
        for piece in range(GROUPS):
            at = part * half + piece * N
            ext[0:8, :N] = hbc[:, at : at + N].astype(F32)[HALO - 8 :]
            ext[8 : 8 + length, :N] = bc_ref[:, at : at + N].astype(F32)
            bcv[part * GROUPS + piece] = convolved(ext, wbc_ref[:, at : at + N], length, N)

    loads[2].wait()

    def columns(k):
        return pl.ds(pl.multiple_of(k * width, 128), width)

    def end_part(k):
        col_i = coli[k]
        ext[0:8, :width] = hx[:, columns(k)].astype(F32)[HALO - 8 :]
        ext[8 : 8 + length, :width] = x_ref[:, columns(k)].astype(F32)
        conv = convolved(ext, wx_ref[:, columns(k)], length, width)
        convs[k] = conv
        weighted = [
            (conv[:, j * P_SIZE : (j + 1) * P_SIZE].astype(F32) * col_i[:, j : j + 1]).astype(BF16)
            for j in range(hs)
        ]
        stacked = jnp.concatenate(weighted, axis=1)
        write = bcv[k * hs // per_group]
        ends[k] = lax.dot_general(stacked, write, TN, preferred_element_type=F32).astype(BF16)

    def intra_part(k):
        group = k * hs // per_group
        scores = lax.dot_general(bcv[GROUPS + group], bcv[group], NT, preferred_element_type=F32)
        col_c, row_c, row_i = colc[k], rowc[k], rowi[k]
        for j in range(hs):
            lanes = slice(j * P_SIZE, (j + 1) * P_SIZE)
            gap = jnp.where(causal, col_c[:, j : j + 1] - row_c[j : j + 1], -jnp.inf)
            mixing = (scores * jnp.exp(gap) * row_i[j : j + 1]).astype(BF16)
            intra[k, :, lanes] = jnp.dot(mixing, convs[k, :, lanes], preferred_element_type=F32)

    def start_part():
        owner = owner_ref[me_b]
        level = level_ref[me_b]
        for step in range(1, nb):
            sel_copy(step).wait_recv()
        state = jnp.where(owner == me_b, start[...], jnp.zeros_like(start))
        for step in range(1, nb):
            state = jnp.where(owner == lax.rem(me_b + nb - step, nb), sel_in[step - 1], state)
        state = jnp.where(level > 0, state, jnp.zeros_like(state))

        @pl.when(me_c == 0)
        def _():
            inc[0] = state

        @pl.when(me_c > 0)
        def _():
            start[...] = state
            for part in range(PARTS):
                start_copy(part).start()

    def chain_part(k):
        decay = jnp.exp(rowc[k][:, length - 1 : length]).astype(BF16).astype(F32)
        for part in range(PARTS):
            @pl.when(me_c + k > 0)
            def _():
                next_copy(k, part).wait_recv()

            @pl.when(me_c < nc - 1)
            def _():
                for j in range(part * hs // PARTS, (part + 1) * hs // PARTS):
                    rows = slice(j * P_SIZE, (j + 1) * P_SIZE)
                    nxt[k, rows] = (
                        decay[j : j + 1] * inc[k, rows].astype(F32) + ends[k, rows].astype(F32)
                    ).astype(BF16)
                next_copy(k, part).start()

    def out_part(k):
        read = bcv[GROUPS + k * hs // per_group]
        inter = lax.dot_general(read, inc[k], NT, preferred_element_type=F32)
        grown = jnp.exp(colc[k])
        gain = gain_ref[:, columns(k)]
        alive = first + lax.broadcasted_iota(jnp.int32, (length, P_SIZE), 0) < live_count
        outs = []
        for j in range(hs):
            lanes = slice(j * P_SIZE, (j + 1) * P_SIZE)
            summed = intra[k, :, lanes] + grown[:, j : j + 1] * inter[:, lanes]
            scale = lax.rsqrt(jnp.mean(summed * summed, axis=1, keepdims=True) + 1e-05)
            outs.append(jnp.where(alive, summed * scale * gain[:, lanes], 0.0).astype(BF16))
        out_ref[:, columns(k)] = jnp.concatenate(outs, axis=1)

    start_at = jnp.where(me_c == 0, 0, nc // 2 - 1)

    def ends_step(k, carry):
        end_part(k)
        pl.when(k == start_at)(start_part)

        @pl.when(me_c == 0)
        def _():
            chain_part(k)

        return carry

    def intra_step(k, carry):
        intra_part(k)
        return carry

    def late_step(k, carry):
        @pl.when(me_c > 0)
        def _():
            chain_part(k)

        @pl.when(me_c < 2)
        def _():
            intra_part(k)

        out_part(k)
        return carry

    lax.fori_loop(0, nc, ends_step, 0)

    @pl.when(me_c >= 2)
    def _():
        lax.fori_loop(0, nc, intra_step, 0)

    lax.fori_loop(0, nc, late_step, 0)

    for step in range(1, nb):
        sel_copy(step).wait_send()

    @pl.when(me_c > 0)
    def _():
        for part in range(PARTS):
            start_copy(part).wait_send()

    @pl.when(me_c < nc - 1)
    def _():
        halo_copy(1).wait_send()
        halo_copy(0).wait_send()

        def drain(k, carry):
            for part in range(PARTS):
                next_copy(k, part).wait_send()
            return carry

        lax.fori_loop(0, nc, drain, 0)


def body(
    nb, nc,
    inner_x, inner_bc, step_size, decay_base, conv_inner, conv_groups, norm_gain, cache_pool,
    reuse_owner, reuse_level, prompt_blocks,
):
    length, width_x = inner_x.shape[1:]
    width_bc = inner_bc.shape[2]
    hs = LOCAL_HEADS // nc
    width = hs * P_SIZE
    smem = pl.BlockSpec(memory_space=pltpu.SMEM)
    vmem = pl.BlockSpec(memory_space=pltpu.VMEM)
    hbm = pl.BlockSpec(memory_space=pl.ANY)
    dma = pltpu.SemaphoreType.DMA
    result = pl.pallas_call(
        functools.partial(kernel, nb, nc, length),
        out_shape=jax.ShapeDtypeStruct((length, width_x), BF16),
        in_specs=[smem] * 3 + [hbm, vmem, vmem, vmem, hbm, vmem, vmem, hbm],
        out_specs=vmem,
        scratch_shapes=[
            pltpu.VMEM((length, width_x), BF16),
            pltpu.VMEM((KCONV, width_x), F32),
            pltpu.VMEM(cache_pool.shape, BF16),
            pltpu.VMEM((nc, length, width), BF16),
            pltpu.VMEM((HALO, width_x), BF16),
            pltpu.VMEM((HALO, width_bc), BF16),
            pltpu.VMEM((8 + length, max(width, N)), F32),
            pltpu.VMEM((2 * GROUPS, length, N), BF16),
            pltpu.VMEM((nc, length, hs), F32),
            pltpu.VMEM((nc, length, hs), F32),
            pltpu.VMEM((nc, hs, length), F32),
            pltpu.VMEM((nc, hs, length), F32),
            pltpu.VMEM((nc, length, width), F32),
            pltpu.VMEM((nc, width, N), BF16),
            pltpu.VMEM((nc, width, N), BF16),
            pltpu.VMEM((nc, width, N), BF16),
            pltpu.VMEM((nb - 1, width, N), BF16),
            pltpu.VMEM((nb - 1, width, N), BF16),
            pltpu.VMEM((width, N), BF16),
            dma((3,)),
            dma((2,)),
            dma((2,)),
            dma((nb - 1,)),
            dma((nb - 1,)),
            dma((PARTS,)),
            dma((nc, PARTS)),
            dma((nc, PARTS)),
        ],
        compiler_params=pltpu.CompilerParams(
            collective_id=0, has_side_effects=True, vmem_limit_bytes=56 * 1024 * 1024
        ),
    )(
        reuse_owner, reuse_level, prompt_blocks,
        inner_x[0], inner_bc[0], step_size[0],
        decay_base[None, :], conv_inner, conv_groups, norm_gain[None, :],
        cache_pool,
    )
    return result[None]


def solution(mesh):
    return jax.shard_map(
        functools.partial(body, mesh.shape["batch"], mesh.shape["ctx"]),
        mesh=mesh,
        in_specs=(
            P("batch", "ctx", None),
            P("batch", "ctx", None),
            P("batch", "ctx", None),
            P(),
            P(),
            P(),
            P(),
            P("batch", "ctx", None, None),
            P(),
            P(),
            P(),
        ),
        out_specs=P("batch", "ctx", None),
        check_vma=False,
    )
```

```python
import functools

import jax
import jax.numpy as jnp
from jax import lax
from jax.experimental import pallas as pl
from jax.experimental.pallas import tpu as pltpu
from jax.sharding import PartitionSpec as P

LOCAL_HEADS = 64
P_SIZE = 128
N = 128
GROUPS = 4
KCONV = 4
LEN_BLOCK = 256
HALO = 16
PARTS = 4
F32 = jnp.float32
BF16 = jnp.bfloat16
MESH = pl.DeviceIdType.MESH
NT = (((1,), (1,)), ((), ()))
TN = (((0,), (0,)), ((), ()))


def one_minus_exp(value):
    total = jnp.ones_like(value)
    for term in range(12, 1, -1):
        total = 1.0 + value * (1.0 / term) * total
    return -value * total


def convolved(ext_ref, weight, length, width):
    summed = jnp.zeros((length, width), F32)
    for offset in range(KCONV):
        start = 8 - (KCONV - 1) + offset
        summed = summed + weight[offset : offset + 1] * ext_ref[start : start + length, :width]
    return (summed * jax.nn.sigmoid(summed)).astype(BF16)


def kernel(
    nb, nc, length,
    owner_ref, level_ref, blocks_ref,
    x_hbm, bc_ref, step_ref, base_ref, wx_hbm, wbc_ref, gain_ref, pool_hbm,
    out_ref,
    x_ref, wx_ref, pool_ref, convs,
    hx, hbc, ext, bcv, colc, coli, rowc, rowi, intra, ends, inc, nxt, sel_out, sel_in, start,
    local_sem, halo_send, halo_recv, sel_send, sel_recv, st_send, inc_recv, nxt_send,
):
    hs = LOCAL_HEADS // nc
    width = hs * P_SIZE
    parts = min(PARTS, hs)
    share = hs // parts
    sub = width // parts
    per_group = LOCAL_HEADS // GROUPS
    me_b = lax.axis_index("batch")
    me_c = lax.axis_index("ctx")
    live_count = blocks_ref[me_b] * LEN_BLOCK

    loads = [
        pltpu.make_async_copy(source, target, local_sem.at[at])
        for at, (source, target) in enumerate(((pool_hbm, pool_ref), (x_hbm, x_ref), (wx_hbm, wx_ref)))
    ]
    for load in loads:
        load.start()
    barrier = pltpu.get_barrier_semaphore()
    for step in range(1, nb):
        pl.semaphore_signal(barrier, inc=1, device_id=(lax.rem(me_b + step, nb), me_c), device_id_type=MESH)
    for step in range(1, nc):
        pl.semaphore_signal(barrier, inc=1, device_id=(me_b, lax.rem(me_c + step, nc)), device_id_type=MESH)

    loads[0].wait()

    def pick(request):
        return pool_ref[jnp.maximum(level_ref[request] - 1, 0)].reshape(width, N)

    for step in range(1, nb):
        sel_out[step - 1] = pick(lax.rem(me_b + step, nb))
    start[...] = pick(me_b)
    loads[1].wait()
    pl.semaphore_wait(barrier, nb - 1 + nc - 1)

    def halo_copy(which):
        source, target = ((x_ref, hx), (bc_ref, hbc))[which]
        return pltpu.make_async_remote_copy(
            src_ref=source.at[pl.ds(length - HALO, HALO)], dst_ref=target,
            send_sem=halo_send.at[which], recv_sem=halo_recv.at[which],
            device_id=(me_b, lax.rem(me_c + 1, nc)), device_id_type=MESH,
        )

    def rows_of(part):
        return pl.ds(pl.multiple_of(part * sub, P_SIZE), sub)

    def sel_copy(step, part):
        return pltpu.make_async_remote_copy(
            src_ref=sel_out.at[step - 1, rows_of(part)], dst_ref=sel_in.at[step - 1, rows_of(part)],
            send_sem=sel_send.at[step - 1, part], recv_sem=sel_recv.at[step - 1, part],
            device_id=(lax.rem(me_b + step, nb), me_c), device_id_type=MESH,
        )

    def start_copy(part):
        rows = rows_of(part)
        return pltpu.make_async_remote_copy(
            src_ref=start.at[rows], dst_ref=inc.at[me_c, rows],
            send_sem=st_send.at[part], recv_sem=inc_recv.at[me_c, part],
            device_id=(me_b, 0), device_id_type=MESH,
        )

    def next_copy(k, part):
        rows = rows_of(part)
        return pltpu.make_async_remote_copy(
            src_ref=nxt.at[k, rows], dst_ref=inc.at[k, rows],
            send_sem=nxt_send.at[k, part], recv_sem=inc_recv.at[k, part],
            device_id=(me_b, lax.rem(me_c + 1, nc)), device_id_type=MESH,
        )

    @pl.when(me_c < nc - 1)
    def _():
        halo_copy(1).start()
        halo_copy(0).start()

    for part in range(parts):
        for step in range(1, nb):
            sel_copy(step, part).start()

    first = me_c * length
    row_at = lax.broadcasted_iota(jnp.int32, (length, LOCAL_HEADS), 0)
    logs = jnp.where(first + row_at < live_count, step_ref[...], 0.0) * jnp.log(base_ref[...])
    at_t = lax.broadcasted_iota(jnp.int32, (length, length), 0)
    at_s = lax.broadcasted_iota(jnp.int32, (length, length), 1)
    causal = at_t >= at_s
    lower = causal.astype(F32)
    upper = (at_t <= at_s).astype(F32)
    cum = jnp.dot(lower, logs, precision=lax.Precision.HIGHEST, preferred_element_type=F32)
    cumt = lax.dot_general(logs, upper, TN, precision=lax.Precision.HIGHEST, preferred_element_type=F32)
    inject = one_minus_exp(logs)
    tail = jnp.exp(cum[length - 1 : length] - cum) * inject
    same = (at_t == at_s).astype(F32)
    injt = lax.dot_general(inject, same, TN, precision=lax.Precision.HIGHEST, preferred_element_type=F32)
    for k in range(nc):
        colc[k] = cum[:, k * hs : (k + 1) * hs]
        coli[k] = tail[:, k * hs : (k + 1) * hs]
        rowc[k] = cumt[k * hs : (k + 1) * hs]
        rowi[k] = injt[k * hs : (k + 1) * hs]

    @pl.when(me_c == 0)
    def _():
        hx[...] = jnp.zeros_like(hx)
        hbc[...] = jnp.zeros_like(hbc)

    @pl.when(me_c > 0)
    def _():
        halo_copy(1).wait_recv()
        halo_copy(0).wait_recv()

    half = GROUPS * N
    for part in range(2):
        cols = slice(part * half, (part + 1) * half)
        for piece in range(GROUPS):
            at = part * half + piece * N
            ext[0:8, :N] = hbc[:, at : at + N].astype(F32)[HALO - 8 :]
            ext[8 : 8 + length, :N] = bc_ref[:, at : at + N].astype(F32)
            bcv[part * GROUPS + piece] = convolved(ext, wbc_ref[:, at : at + N], length, N)

    loads[2].wait()

    def columns(k):
        return pl.ds(pl.multiple_of(k * width, 128), width)

    def end_part(k):
        col_i = coli[k]
        ext[0:8, :width] = hx[:, columns(k)].astype(F32)[HALO - 8 :]
        ext[8 : 8 + length, :width] = x_ref[:, columns(k)].astype(F32)
        conv = convolved(ext, wx_ref[:, columns(k)], length, width)
        convs[k] = conv
        weighted = [
            (conv[:, j * P_SIZE : (j + 1) * P_SIZE].astype(F32) * col_i[:, j : j + 1]).astype(BF16)
            for j in range(hs)
        ]
        stacked = jnp.concatenate(weighted, axis=1)
        write = bcv[k * hs // per_group]
        ends[k] = lax.dot_general(stacked, write, TN, preferred_element_type=F32).astype(BF16)

    def intra_part(k):
        group = k * hs // per_group
        scores = lax.dot_general(bcv[GROUPS + group], bcv[group], NT, preferred_element_type=F32)
        col_c, row_c, row_i = colc[k], rowc[k], rowi[k]
        for j in range(hs):
            lanes = slice(j * P_SIZE, (j + 1) * P_SIZE)
            gap = jnp.where(causal, col_c[:, j : j + 1] - row_c[j : j + 1], -jnp.inf)
            mixing = (scores * jnp.exp(gap) * row_i[j : j + 1]).astype(BF16)
            intra[k, :, lanes] = jnp.dot(mixing, convs[k, :, lanes], preferred_element_type=F32)

    def start_part(part):
        owner = owner_ref[me_b]
        level = level_ref[me_b]
        rows = rows_of(part)
        for step in range(1, nb):
            sel_copy(step, part).wait_recv()
        mine = start[rows]
        state = jnp.where(owner == me_b, mine, jnp.zeros_like(mine))
        for step in range(1, nb):
            state = jnp.where(owner == lax.rem(me_b + nb - step, nb), sel_in[step - 1, rows], state)
        state = jnp.where(level > 0, state, jnp.zeros_like(state))

        @pl.when(me_c == 0)
        def _():
            inc[0, rows] = state

        @pl.when(me_c > 0)
        def _():
            start[rows] = state
            start_copy(part).start()

    def chain_part(k, part):
        @pl.when(me_c + k > 0)
        def _():
            next_copy(k, part).wait_recv()

        @pl.when(me_c < nc - 1)
        def _():
            decay = jnp.exp(rowc[k][:, length - 1 : length]).astype(BF16).astype(F32)
            for j in range(part * share, (part + 1) * share):
                rows = slice(j * P_SIZE, (j + 1) * P_SIZE)
                nxt[k, rows] = (
                    decay[j : j + 1] * inc[k, rows].astype(F32) + ends[k, rows].astype(F32)
                ).astype(BF16)
            next_copy(k, part).start()

    def out_part(k, part):
        read = bcv[GROUPS + k * hs // per_group]
        inter = lax.dot_general(
            read, inc[k, part * sub : (part + 1) * sub], NT, preferred_element_type=F32
        )
        grown = jnp.exp(colc[k])
        cols = pl.ds(pl.multiple_of(k * width + part * sub, P_SIZE), sub)
        gain = gain_ref[:, cols]
        alive = first + lax.broadcasted_iota(jnp.int32, (length, P_SIZE), 0) < live_count
        outs = []
        for at in range(share):
            j = part * share + at
            lanes = slice(at * P_SIZE, (at + 1) * P_SIZE)
            summed = (
                intra[k, :, j * P_SIZE : (j + 1) * P_SIZE] + grown[:, j : j + 1] * inter[:, lanes]
            )
            scale = lax.rsqrt(jnp.mean(summed * summed, axis=1, keepdims=True) + 1e-05)
            outs.append(jnp.where(alive, summed * scale * gain[:, lanes], 0.0).astype(BF16))
        out_ref[:, cols] = jnp.concatenate(outs, axis=1)

    def ends_step(k, carry):
        end_part(k)
        return carry

    def intra_step(k, carry):
        intra_part(k)
        return carry

    def late_step(part, k, carry):
        def serve(later, inner):
            @pl.when(part * nc + k == jnp.maximum(6 * later - 2 * me_c, 0))
            def _():
                start_part(later)

            return inner

        if part < parts - 1:
            lax.fori_loop(1, parts, serve, 0)
        chain_part(k, part)
        if part == 0:
            @pl.when(me_c < 2)
            def _():
                intra_part(k)

        out_part(k, part)
        return carry

    lax.fori_loop(0, nc, ends_step, 0)
    start_part(0)

    @pl.when(me_c >= 2)
    def _():
        lax.fori_loop(0, nc, intra_step, 0)

    for part in range(parts):
        lax.fori_loop(0, nc, functools.partial(late_step, part), 0)

    for part in range(parts):
        for step in range(1, nb):
            sel_copy(step, part).wait_send()

    @pl.when(me_c > 0)
    def _():
        for part in range(parts):
            start_copy(part).wait_send()

    @pl.when(me_c < nc - 1)
    def _():
        halo_copy(1).wait_send()
        halo_copy(0).wait_send()

        def drain(k, carry):
            for part in range(parts):
                next_copy(k, part).wait_send()
            return carry

        lax.fori_loop(0, nc, drain, 0)


def body(
    nb, nc,
    inner_x, inner_bc, step_size, decay_base, conv_inner, conv_groups, norm_gain, cache_pool,
    reuse_owner, reuse_level, prompt_blocks,
):
    length, width_x = inner_x.shape[1:]
    width_bc = inner_bc.shape[2]
    hs = LOCAL_HEADS // nc
    width = hs * P_SIZE
    parts = min(PARTS, hs)
    smem = pl.BlockSpec(memory_space=pltpu.SMEM)
    vmem = pl.BlockSpec(memory_space=pltpu.VMEM)
    hbm = pl.BlockSpec(memory_space=pl.ANY)
    dma = pltpu.SemaphoreType.DMA
    result = pl.pallas_call(
        functools.partial(kernel, nb, nc, length),
        out_shape=jax.ShapeDtypeStruct((length, width_x), BF16),
        in_specs=[smem] * 3 + [hbm, vmem, vmem, vmem, hbm, vmem, vmem, hbm],
        out_specs=vmem,
        scratch_shapes=[
            pltpu.VMEM((length, width_x), BF16),
            pltpu.VMEM((KCONV, width_x), F32),
            pltpu.VMEM(cache_pool.shape, BF16),
            pltpu.VMEM((nc, length, width), BF16),
            pltpu.VMEM((HALO, width_x), BF16),
            pltpu.VMEM((HALO, width_bc), BF16),
            pltpu.VMEM((8 + length, max(width, N)), F32),
            pltpu.VMEM((2 * GROUPS, length, N), BF16),
            pltpu.VMEM((nc, length, hs), F32),
            pltpu.VMEM((nc, length, hs), F32),
            pltpu.VMEM((nc, hs, length), F32),
            pltpu.VMEM((nc, hs, length), F32),
            pltpu.VMEM((nc, length, width), F32),
            pltpu.VMEM((nc, width, N), BF16),
            pltpu.VMEM((nc, width, N), BF16),
            pltpu.VMEM((nc, width, N), BF16),
            pltpu.VMEM((nb - 1, width, N), BF16),
            pltpu.VMEM((nb - 1, width, N), BF16),
            pltpu.VMEM((width, N), BF16),
            dma((3,)),
            dma((2,)),
            dma((2,)),
            dma((nb - 1, parts)),
            dma((nb - 1, parts)),
            dma((parts,)),
            dma((nc, parts)),
            dma((nc, parts)),
        ],
        compiler_params=pltpu.CompilerParams(
            collective_id=0, has_side_effects=True, vmem_limit_bytes=56 * 1024 * 1024
        ),
    )(
        reuse_owner, reuse_level, prompt_blocks,
        inner_x[0], inner_bc[0], step_size[0],
        decay_base[None, :], conv_inner, conv_groups, norm_gain[None, :],
        cache_pool,
    )
    return result[None]


def solution(mesh):
    return jax.shard_map(
        functools.partial(body, mesh.shape["batch"], mesh.shape["ctx"]),
        mesh=mesh,
        in_specs=(
            P("batch", "ctx", None),
            P("batch", "ctx", None),
            P("batch", "ctx", None),
            P(),
            P(),
            P(),
            P(),
            P("batch", "ctx", None, None),
            P(),
            P(),
            P(),
        ),
        out_specs=P("batch", "ctx", None),
        check_vma=False,
    )
```

```python
import functools

import jax
import jax.numpy as jnp
from jax import lax
from jax.experimental import pallas as pl
from jax.experimental.pallas import tpu as pltpu
from jax.sharding import PartitionSpec as P

LOCAL_HEADS = 64
P_SIZE = 128
N = 128
GROUPS = 4
KCONV = 4
LEN_BLOCK = 256
HALO = 16
PARTS = 4
F32 = jnp.float32
BF16 = jnp.bfloat16
MESH = pl.DeviceIdType.MESH
NT = (((1,), (1,)), ((), ()))
TN = (((0,), (0,)), ((), ()))


def one_minus_exp(value):
    total = jnp.ones_like(value)
    for term in range(12, 1, -1):
        total = 1.0 + value * (1.0 / term) * total
    return -value * total


def convolved(ext_ref, weight, length, width):
    summed = jnp.zeros((length, width), F32)
    for offset in range(KCONV):
        start = 8 - (KCONV - 1) + offset
        summed = summed + weight[offset : offset + 1] * ext_ref[start : start + length, :width]
    return (summed * jax.nn.sigmoid(summed)).astype(BF16)


def kernel(
    nb, nc, length,
    owner_ref, level_ref, blocks_ref,
    x_hbm, bc_hbm, step_ref, base_ref, wx_hbm, wbc_hbm, gain_hbm, pool_hbm,
    out_hbm,
    x_ref, wx_ref, pool_ref, convs, bc_ref, wbc_ref, gain_ref, out_ref, out_sem,
    hx, hbc, ext, bcv, colc, coli, rowc, rowi, intra, ends, inc, nxt, sel_out, sel_in, start,
    local_sem, halo_send, halo_recv, sel_send, sel_recv, st_send, inc_recv, nxt_send,
):
    hs = LOCAL_HEADS // nc
    width = hs * P_SIZE
    parts = min(PARTS, hs)
    share = hs // parts
    sub = width // parts
    per_group = LOCAL_HEADS // GROUPS
    me_b = lax.axis_index("batch")
    me_c = lax.axis_index("ctx")
    live_count = blocks_ref[me_b] * LEN_BLOCK

    loads = [
        pltpu.make_async_copy(source, target, local_sem.at[at])
        for at, (source, target) in enumerate((
            (pool_hbm, pool_ref), (x_hbm, x_ref), (bc_hbm, bc_ref),
            (wbc_hbm, wbc_ref), (wx_hbm, wx_ref), (gain_hbm, gain_ref),
        ))
    ]
    for load in loads:
        load.start()
    barrier = pltpu.get_barrier_semaphore()
    for step in range(1, nb):
        pl.semaphore_signal(barrier, inc=1, device_id=(lax.rem(me_b + step, nb), me_c), device_id_type=MESH)
    for step in range(1, nc):
        pl.semaphore_signal(barrier, inc=1, device_id=(me_b, lax.rem(me_c + step, nc)), device_id_type=MESH)

    loads[0].wait()

    def pick(request):
        return pool_ref[jnp.maximum(level_ref[request] - 1, 0)].reshape(width, N)

    for step in range(1, nb):
        sel_out[step - 1] = pick(lax.rem(me_b + step, nb))
    start[...] = pick(me_b)
    loads[1].wait()
    loads[2].wait()
    pl.semaphore_wait(barrier, nb - 1 + nc - 1)

    def halo_copy(which):
        source, target = ((x_ref, hx), (bc_ref, hbc))[which]
        return pltpu.make_async_remote_copy(
            src_ref=source.at[pl.ds(length - HALO, HALO)], dst_ref=target,
            send_sem=halo_send.at[which], recv_sem=halo_recv.at[which],
            device_id=(me_b, lax.rem(me_c + 1, nc)), device_id_type=MESH,
        )

    def rows_of(part):
        return pl.ds(pl.multiple_of(part * sub, P_SIZE), sub)

    def sel_copy(step, part):
        return pltpu.make_async_remote_copy(
            src_ref=sel_out.at[step - 1, rows_of(part)], dst_ref=sel_in.at[step - 1, rows_of(part)],
            send_sem=sel_send.at[step - 1, part], recv_sem=sel_recv.at[step - 1, part],
            device_id=(lax.rem(me_b + step, nb), me_c), device_id_type=MESH,
        )

    def start_copy(part):
        rows = rows_of(part)
        return pltpu.make_async_remote_copy(
            src_ref=start.at[rows], dst_ref=inc.at[me_c, rows],
            send_sem=st_send.at[part], recv_sem=inc_recv.at[me_c, part],
            device_id=(me_b, 0), device_id_type=MESH,
        )

    def next_copy(k, part):
        rows = rows_of(part)
        return pltpu.make_async_remote_copy(
            src_ref=nxt.at[k, rows], dst_ref=inc.at[k, rows],
            send_sem=nxt_send.at[k, part], recv_sem=inc_recv.at[k, part],
            device_id=(me_b, lax.rem(me_c + 1, nc)), device_id_type=MESH,
        )

    @pl.when(me_c < nc - 1)
    def _():
        halo_copy(1).start()
        halo_copy(0).start()

    for part in range(parts):
        for step in range(1, nb):
            sel_copy(step, part).start()

    first = me_c * length
    row_at = lax.broadcasted_iota(jnp.int32, (length, LOCAL_HEADS), 0)
    logs = jnp.where(first + row_at < live_count, step_ref[...], 0.0) * jnp.log(base_ref[...])
    at_t = lax.broadcasted_iota(jnp.int32, (length, length), 0)
    at_s = lax.broadcasted_iota(jnp.int32, (length, length), 1)
    causal = at_t >= at_s
    lower = causal.astype(F32)
    upper = (at_t <= at_s).astype(F32)
    cum = jnp.dot(lower, logs, precision=lax.Precision.HIGHEST, preferred_element_type=F32)
    cumt = lax.dot_general(logs, upper, TN, precision=lax.Precision.HIGHEST, preferred_element_type=F32)
    inject = one_minus_exp(logs)
    tail = jnp.exp(cum[length - 1 : length] - cum) * inject
    same = (at_t == at_s).astype(F32)
    injt = lax.dot_general(inject, same, TN, precision=lax.Precision.HIGHEST, preferred_element_type=F32)
    for k in range(nc):
        colc[k] = cum[:, k * hs : (k + 1) * hs]
        coli[k] = tail[:, k * hs : (k + 1) * hs]
        rowc[k] = cumt[k * hs : (k + 1) * hs]
        rowi[k] = injt[k * hs : (k + 1) * hs]

    @pl.when(me_c == 0)
    def _():
        hx[...] = jnp.zeros_like(hx)
        hbc[...] = jnp.zeros_like(hbc)

    @pl.when(me_c > 0)
    def _():
        halo_copy(1).wait_recv()
        halo_copy(0).wait_recv()

    loads[3].wait()
    half = GROUPS * N
    for part in range(2):
        cols = slice(part * half, (part + 1) * half)
        for piece in range(GROUPS):
            at = part * half + piece * N
            ext[0:8, :N] = hbc[:, at : at + N].astype(F32)[HALO - 8 :]
            ext[8 : 8 + length, :N] = bc_ref[:, at : at + N].astype(F32)
            bcv[part * GROUPS + piece] = convolved(ext, wbc_ref[:, at : at + N], length, N)

    loads[4].wait()
    loads[5].wait()

    def columns(k):
        return pl.ds(pl.multiple_of(k * width, 128), width)

    def end_part(k):
        col_i = coli[k]
        ext[0:8, :width] = hx[:, columns(k)].astype(F32)[HALO - 8 :]
        ext[8 : 8 + length, :width] = x_ref[:, columns(k)].astype(F32)
        conv = convolved(ext, wx_ref[:, columns(k)], length, width)
        convs[k] = conv
        weighted = [
            (conv[:, j * P_SIZE : (j + 1) * P_SIZE].astype(F32) * col_i[:, j : j + 1]).astype(BF16)
            for j in range(hs)
        ]
        stacked = jnp.concatenate(weighted, axis=1)
        write = bcv[k * hs // per_group]
        ends[k] = lax.dot_general(stacked, write, TN, preferred_element_type=F32).astype(BF16)

    def intra_part(k):
        group = k * hs // per_group
        scores = lax.dot_general(bcv[GROUPS + group], bcv[group], NT, preferred_element_type=F32)
        col_c, row_c, row_i = colc[k], rowc[k], rowi[k]
        for j in range(hs):
            lanes = slice(j * P_SIZE, (j + 1) * P_SIZE)
            gap = jnp.where(causal, col_c[:, j : j + 1] - row_c[j : j + 1], -jnp.inf)
            mixing = (scores * jnp.exp(gap) * row_i[j : j + 1]).astype(BF16)
            intra[k, :, lanes] = jnp.dot(mixing, convs[k, :, lanes], preferred_element_type=F32)

    def start_part(part):
        owner = owner_ref[me_b]
        level = level_ref[me_b]
        rows = rows_of(part)
        for step in range(1, nb):
            sel_copy(step, part).wait_recv()
        mine = start[rows]
        state = jnp.where(owner == me_b, mine, jnp.zeros_like(mine))
        for step in range(1, nb):
            state = jnp.where(owner == lax.rem(me_b + nb - step, nb), sel_in[step - 1, rows], state)
        state = jnp.where(level > 0, state, jnp.zeros_like(state))

        @pl.when(me_c == 0)
        def _():
            inc[0, rows] = state

        @pl.when(me_c > 0)
        def _():
            start[rows] = state
            start_copy(part).start()

    def chain_part(k, part):
        @pl.when(me_c + k > 0)
        def _():
            next_copy(k, part).wait_recv()

        @pl.when(me_c < nc - 1)
        def _():
            decay = jnp.exp(rowc[k][:, length - 1 : length]).astype(BF16).astype(F32)
            for j in range(part * share, (part + 1) * share):
                rows = slice(j * P_SIZE, (j + 1) * P_SIZE)
                nxt[k, rows] = (
                    decay[j : j + 1] * inc[k, rows].astype(F32) + ends[k, rows].astype(F32)
                ).astype(BF16)
            next_copy(k, part).start()

    def out_copy(k, part):
        cols = pl.ds(pl.multiple_of(k * width + part * sub, P_SIZE), sub)
        return pltpu.make_async_copy(out_ref.at[:, cols], out_hbm.at[:, cols], out_sem.at[k, part])

    def out_part(k, part):
        read = bcv[GROUPS + k * hs // per_group]
        inter = lax.dot_general(
            read, inc[k, part * sub : (part + 1) * sub], NT, preferred_element_type=F32
        )
        grown = jnp.exp(colc[k])
        cols = pl.ds(pl.multiple_of(k * width + part * sub, P_SIZE), sub)
        gain = gain_ref[:, cols]
        alive = first + lax.broadcasted_iota(jnp.int32, (length, P_SIZE), 0) < live_count
        outs = []
        for at in range(share):
            j = part * share + at
            lanes = slice(at * P_SIZE, (at + 1) * P_SIZE)
            summed = (
                intra[k, :, j * P_SIZE : (j + 1) * P_SIZE] + grown[:, j : j + 1] * inter[:, lanes]
            )
            scale = lax.rsqrt(jnp.mean(summed * summed, axis=1, keepdims=True) + 1e-05)
            outs.append(jnp.where(alive, summed * scale * gain[:, lanes], 0.0).astype(BF16))
        out_ref[:, cols] = jnp.concatenate(outs, axis=1)
        out_copy(k, part).start()

    def ends_step(k, carry):
        end_part(k)
        return carry

    def intra_step(k, carry):
        intra_part(k)
        return carry

    def late_step(part, k, carry):
        def serve(later, inner):
            @pl.when(part * nc + k == jnp.maximum(6 * later - 2 * me_c, 0))
            def _():
                start_part(later)

            return inner

        if part < parts - 1:
            lax.fori_loop(1, parts, serve, 0)
        chain_part(k, part)
        if part == 0:
            @pl.when(me_c < 2)
            def _():
                intra_part(k)

        out_part(k, part)
        return carry

    lax.fori_loop(0, nc, ends_step, 0)
    start_part(0)

    @pl.when(me_c >= 2)
    def _():
        lax.fori_loop(0, nc, intra_step, 0)

    for part in range(parts):
        lax.fori_loop(0, nc, functools.partial(late_step, part), 0)

    for part in range(parts):
        for step in range(1, nb):
            sel_copy(step, part).wait_send()

    @pl.when(me_c > 0)
    def _():
        for part in range(parts):
            start_copy(part).wait_send()

    @pl.when(me_c < nc - 1)
    def _():
        halo_copy(1).wait_send()
        halo_copy(0).wait_send()

        def drain(k, carry):
            for part in range(parts):
                next_copy(k, part).wait_send()
            return carry

        lax.fori_loop(0, nc, drain, 0)

    def finish(k, carry):
        for part in range(parts):
            out_copy(k, part).wait()
        return carry

    lax.fori_loop(0, nc, finish, 0)


def body(
    nb, nc,
    inner_x, inner_bc, step_size, decay_base, conv_inner, conv_groups, norm_gain, cache_pool,
    reuse_owner, reuse_level, prompt_blocks,
):
    length, width_x = inner_x.shape[1:]
    width_bc = inner_bc.shape[2]
    hs = LOCAL_HEADS // nc
    width = hs * P_SIZE
    parts = min(PARTS, hs)
    smem = pl.BlockSpec(memory_space=pltpu.SMEM)
    vmem = pl.BlockSpec(memory_space=pltpu.VMEM)
    hbm = pl.BlockSpec(memory_space=pl.ANY)
    dma = pltpu.SemaphoreType.DMA
    result = pl.pallas_call(
        functools.partial(kernel, nb, nc, length),
        out_shape=jax.ShapeDtypeStruct((length, width_x), BF16),
        in_specs=[smem] * 3 + [hbm, hbm, vmem, vmem, hbm, hbm, hbm, hbm],
        out_specs=hbm,
        scratch_shapes=[
            pltpu.VMEM((length, width_x), BF16),
            pltpu.VMEM((KCONV, width_x), F32),
            pltpu.VMEM(cache_pool.shape, BF16),
            pltpu.VMEM((nc, length, width), BF16),
            pltpu.VMEM((length, width_bc), BF16),
            pltpu.VMEM((KCONV, width_bc), F32),
            pltpu.VMEM((1, width_x), F32),
            pltpu.VMEM((length, width_x), BF16),
            dma((nc, parts)),
            pltpu.VMEM((HALO, width_x), BF16),
            pltpu.VMEM((HALO, width_bc), BF16),
            pltpu.VMEM((8 + length, max(width, N)), F32),
            pltpu.VMEM((2 * GROUPS, length, N), BF16),
            pltpu.VMEM((nc, length, hs), F32),
            pltpu.VMEM((nc, length, hs), F32),
            pltpu.VMEM((nc, hs, length), F32),
            pltpu.VMEM((nc, hs, length), F32),
            pltpu.VMEM((nc, length, width), F32),
            pltpu.VMEM((nc, width, N), BF16),
            pltpu.VMEM((nc, width, N), BF16),
            pltpu.VMEM((nc, width, N), BF16),
            pltpu.VMEM((nb - 1, width, N), BF16),
            pltpu.VMEM((nb - 1, width, N), BF16),
            pltpu.VMEM((width, N), BF16),
            dma((6,)),
            dma((2,)),
            dma((2,)),
            dma((nb - 1, parts)),
            dma((nb - 1, parts)),
            dma((parts,)),
            dma((nc, parts)),
            dma((nc, parts)),
        ],
        compiler_params=pltpu.CompilerParams(
            collective_id=0, has_side_effects=True, vmem_limit_bytes=56 * 1024 * 1024
        ),
    )(
        reuse_owner, reuse_level, prompt_blocks,
        inner_x[0], inner_bc[0], step_size[0],
        decay_base[None, :], conv_inner, conv_groups, norm_gain[None, :],
        cache_pool,
    )
    return result[None]


def solution(mesh):
    return jax.shard_map(
        functools.partial(body, mesh.shape["batch"], mesh.shape["ctx"]),
        mesh=mesh,
        in_specs=(
            P("batch", "ctx", None),
            P("batch", "ctx", None),
            P("batch", "ctx", None),
            P(),
            P(),
            P(),
            P(),
            P("batch", "ctx", None, None),
            P(),
            P(),
            P(),
        ),
        out_specs=P("batch", "ctx", None),
        check_vma=False,
    )
```
